256 devices in a mesh: expert: 16 (over x_lo, z), tensor: 8 (over y, x_hi), pair: 2 (over core).
Axes of the slice: x: 4 (x_hi: 2, x_lo: 2; x = x_hi * 2 + x_lo), y: 4, z: 8, core: 2. Of those that a mesh axis runs over, the one named last changes fastest.
Arguments:
- context: bfloat16 [2048, 4096], P('expert', 'tensor'), may hold values from -6 to 6
- out_weight: bfloat16 [4096, 4096], P('tensor', 'pair'), may hold values from -0.09375 to 0.09375
- residual: bfloat16 [2048, 4096], P(('expert', 'tensor'), 'pair'), may hold values from -6 to 6
- norm_gain: bfloat16 [4096], replicated, may hold values from 0.099609375 to 1.8984375
- expert_ids: int32 [2048, 8], P(('expert', 'tensor')), may hold values from 0 to 127, all different within a row; in each aligned block of 16 rows (0 to 15, 16 to 31, ...) at most 2 rows name the same one
- route_prob: float32 [2048, 8], P(('expert', 'tensor')), may hold values from 0.02 to 1
- w_gate: bfloat16 [128, 4096, 768], P(('expert', 'tensor'), None, 'pair'), may hold values from -0.09375 to 0.09375
- w_up: bfloat16 [128, 4096, 768], P(('expert', 'tensor'), None, 'pair'), may hold values from -0.09375 to 0.09375
- w_down: bfloat16 [128, 768, 4096], P(('expert', 'tensor'), 'pair'), may hold values from -0.21875 to 0.21875
Outputs:
- layer_out: bfloat16 [2048, 4096], P(('expert', 'tensor'), 'pair')
The draws below stay inside these ranges and needn't reach their ends.
Inputs may be any that keep to these rules, and one draw needn't show every extreme that they name: `expert_ids`: each row names 8 different experts. In each aligned block of 16 rows (the rows of one device) no expert is named by more than 2 rows, a bound that some block reaches.
All inputs are finite; a program needn't handle non-finite values.
Results may differ from the reference program's by a relative error of at most 0.0052.
Values may be sent and summed in bfloat16 or wider, within the bound.
A program may use at most 64 MiB of HBM per device.

```python
import math
import jax
import jax.numpy as jnp
import numpy as np
from jax import lax

D = 4096
HEAD_DIM = 128
TOP = 8
HEADS = 32
FF = 768
TOKENS = 2048
ROWS = 16
EXPERTS = 128
CAP = 2
HALVES = 2


def shard_levels(rng, dims, pieces, low, top_value):
    gain, own = 1.0, jax.random.fold_in(rng, 6)
    for axis_at, shards_of in pieces:
        steps = jnp.exp(jax.random.uniform(jax.random.fold_in(own, axis_at), (shards_of,), jnp.float32, low / len(pieces), top_value / len(pieces)))
        gain = gain * jnp.repeat(steps, dims[axis_at] // shards_of).reshape([-1 if axis == axis_at else 1 for axis in range(len(dims))])
    return gain


def deal_out(rng, own, number, rows, count, top, reach, lean):
    ranking = jax.random.permutation(rng, count)
    packed, common = load_shares(count, rows * top, reach, lean, True), load_shares(count, rows * top, reach, lean, False)
    places = jnp.arange(count)

    def named(sizes, offset_by):
        used = int((sizes > 0).sum())
        fixed = max(1, used // 4)
        passed = fixed + (places - fixed + offset_by * (used - fixed)) % max(1, count - fixed)
        return jnp.zeros((count,), jnp.int32).at[ranking[jnp.where(places < fixed, places, passed)]].set(jnp.asarray(sizes, jnp.int32))

    sizes = jnp.where(number % 4 == 0, named(packed, number // 4), named(common, number - number // 4 - 1))
    mixed = jax.random.permutation(jax.random.fold_in(own, 3), count)
    giver, taker = mixed[0:count // 2 * 2:2], mixed[1:count // 2 * 2:2]
    slack = jnp.minimum(sizes[giver] - 1, reach - sizes[taker]) // 2
    slack = jnp.where((giver == ranking[0]) | (taker == ranking[0]) | (sizes[taker] == 0), 0, jnp.maximum(slack, 0))
    passed = jax.random.randint(jax.random.fold_in(own, 4), (count // 2,), 0, 1 << 20) % (slack + 1)
    sizes = sizes.at[giver].add(-passed).at[taker].add(passed)
    labels = jnp.searchsorted(jnp.cumsum(sizes), jnp.arange(rows * top), side="right").astype(jnp.int32)
    grid = labels.reshape(top, rows).T
    grid = grid[jax.random.permutation(jax.random.fold_in(own, 1), rows)]
    offset_by = jax.random.randint(jax.random.fold_in(own, 2), (rows, 1), 0, top)
    return jnp.take_along_axis(grid, (jnp.arange(top)[None, :] + offset_by) % top, axis=1)


def load_shares(amount, total, limit, skew, full):
    portions = [(1 << 20) // math.isqrt(rank ** skew) + 1 for rank in range(1, amount + 1)]
    largest = limit if full else min(limit, max(-(-total // amount), total * portions[0] // sum(portions)))
    least = 1 if total - largest >= amount - 1 else 0
    counts, spare = [largest] + [least] * (amount - 1), total - largest - least * (amount - 1)
    while spare > 0:
        free = [i for i in range(1, amount) if counts[i] < largest] or [i for i in range(1, amount) if counts[i] < limit]
        whole, left = sum([portions[i] for i in free]), spare
        for i in free:
            addition = min(limit - counts[i], max(1, left * portions[i] // whole), spare)
            counts[i] = counts[i] + addition
            spare = spare - addition
    return np.array(counts)


def scatter_about(stream_key, extent, deviation, reach, split=(), kind=jnp.bfloat16):
    loudness = shard_levels(stream_key, extent, split, -0.22, 0.18) if split else 1.0
    array = jax.random.normal(stream_key, extent, jnp.float32) * deviation * loudness
    return jnp.minimum(jnp.maximum(array, -reach), reach).astype(kind)


def setup_inputs(seed: int = 0) -> dict:
    seeds = jax.random.split(jax.random.key(seed), 10)
    context = scatter_about(seeds[0], (TOKENS, HEADS * HEAD_DIM), 1.0, 6.0, ((0, 16), (1, 8)))
    out_weight = scatter_about(seeds[1], (HEADS * HEAD_DIM, D), (HEADS * HEAD_DIM) ** -0.5, 0.09375, ((0, 8), (1, 2)))
    residual = scatter_about(seeds[2], (TOKENS, D), 1.0, 6.0, ((0, 128), (1, 2)))
    norm_gain = jnp.clip(1.0 + 0.18 * jax.random.normal(seeds[3], (D,), jnp.float32), 0.099609375, 1.8984375).astype(jnp.bfloat16)
    expert_ids_keys = jax.random.split(jax.random.fold_in(seeds[4], 1), TOKENS // ROWS)
    expert_ids_turns = jax.random.permutation(jax.random.fold_in(seeds[4], 3), TOKENS // ROWS)
    expert_ids = jax.vmap(lambda own, number: deal_out(jax.random.fold_in(seeds[4], 2), own, number, ROWS, EXPERTS, TOP, CAP, 1))(expert_ids_keys, expert_ids_turns).reshape((TOKENS, TOP))
    route_prob = jnp.clip(jnp.exp(math.log(1.0) - 3.912023 * jax.random.uniform(seeds[5], (TOKENS, TOP), jnp.float32) ** shard_levels(seeds[5], (TOKENS, TOP), ((0, 128),), -0.2, 0.2)), 0.02, 1.0)
    w_gate = scatter_about(seeds[6], (EXPERTS, D, FF), D ** -0.5, 0.09375, ((0, 128), (2, 2)))
    w_up = scatter_about(seeds[7], (EXPERTS, D, FF), D ** -0.5, 0.09375, ((0, 128), (2, 2)))
    w_down = scatter_about(seeds[8], (EXPERTS, FF, D), FF ** -0.5, 0.21875, ((0, 128), (1, 2)))
    return {"context": context, "out_weight": out_weight, "residual": residual, "norm_gain": norm_gain, "expert_ids": expert_ids, "route_prob": route_prob, "w_gate": w_gate, "w_up": w_up, "w_down": w_down}


EPS = 1e-06

def reference(context, out_weight, residual, norm_gain, expert_ids, route_prob, w_gate, w_up, w_down):
    attention_output = jnp.dot(context, out_weight, preferred_element_type=jnp.float32)
    stream = (residual.astype(jnp.float32) + attention_output).astype(jnp.bfloat16)
    widened = stream.astype(jnp.float32)
    norm_scale = lax.rsqrt(lax.optimization_barrier(jnp.mean(widened * widened, axis=1, keepdims=True)) + EPS)
    normed = (widened * norm_scale * norm_gain.astype(jnp.float32)).astype(jnp.bfloat16)
    block_count = TOKENS // ROWS
    flat_ids = expert_ids.reshape(block_count, ROWS * TOP).astype(jnp.int32)
    expert_marks = (flat_ids[:, :, None] == jnp.arange(EXPERTS, dtype=jnp.int32)[None, None, :]).astype(jnp.int32)
    slot_index = lax.optimization_barrier(jnp.sum((jnp.cumsum(expert_marks, axis=1) - expert_marks) * expert_marks, axis=2)).astype(jnp.int32)
    block_index = jnp.broadcast_to(jnp.arange(block_count, dtype=jnp.int32)[:, None], flat_ids.shape)
    source_rows = jnp.repeat(normed.reshape(block_count, ROWS, D), TOP, axis=1)
    dispatched_tokens = jnp.zeros((EXPERTS, block_count, CAP, D), jnp.bfloat16)
    dispatched_tokens = dispatched_tokens.at[flat_ids, block_index, slot_index].set(source_rows)

    def run_expert(item):
        rows_in, gate_weight, up_weight, down_weight = item
        flat_rows = rows_in.reshape(block_count * CAP, D).astype(jnp.float32)
        gate_values = jnp.dot(flat_rows, gate_weight.astype(jnp.float32))
        up_values = jnp.dot(flat_rows, up_weight.astype(jnp.float32))
        hidden = (jax.nn.silu(gate_values) * up_values).astype(jnp.bfloat16)
        expert_pieces = hidden.reshape(block_count * CAP, HALVES, FF // HALVES).astype(jnp.float32)
        down_projection_parts = down_weight.reshape(HALVES, FF // HALVES, D).astype(jnp.float32)
        partial_sums = jnp.einsum('lwc,wce->wle', expert_pieces, down_projection_parts).astype(jnp.bfloat16)
        partial_sums = lax.optimization_barrier(partial_sums).astype(jnp.float32)
        return lax.optimization_barrier(jnp.sum(partial_sums, axis=0)).astype(jnp.bfloat16).reshape(block_count, CAP, D)
    expert_out = lax.map(run_expert, (dispatched_tokens, w_gate, w_up, w_down))
    picked = expert_out[flat_ids, block_index, slot_index].reshape(TOKENS, TOP, D).astype(jnp.float32)
    weights = route_prob / lax.optimization_barrier(jnp.sum(route_prob, axis=1, keepdims=True))
    mixture = lax.optimization_barrier(jnp.sum(weights[:, :, None] * picked, axis=1))
    return (stream.astype(jnp.float32) + mixture).astype(jnp.bfloat16)
```

```python
import functools

import jax
import jax.numpy as jnp
from jax import lax
from jax.experimental import pallas as pl
from jax.experimental.pallas import tpu as pltpu
from jax.sharding import PartitionSpec as P

EPS = 1e-06
MESH = pl.DeviceIdType.MESH
BF16 = jnp.bfloat16
F32 = jnp.float32
ROWS = 16
NZ = 8
NT = 8
NQ = 16
CHUNKS = 4


def dot(a, b):
    return jnp.dot(a, b, preferred_element_type=F32)


def dot_nt(a, b):
    return lax.dot_general(a, b, (((1,), (1,)), ((), ())), preferred_element_type=F32)


def rows16(index):
    return pl.ds(pl.multiple_of(index * ROWS, ROWS), ROWS)


def kernel(
    ctx_hbm, ow_hbm, res_hbm, gain_hbm, ids_hbm, prob_hbm, wg_hbm, wu_hbm, wd_hbm, out_ref,
    ctx, ow, res, gain, ids, prob, wgu, wd,
    attb, ars, stream, ssq, meta, metal, table, chi, clo,
    line, disp, xs, acc, hid, outb, ret, mixb, zr,
    ld, ow_sem, w_sem,
    a_send, a_recv, m_sem, wd_sem, s_sem, g_send, g_recv, d_send, d_recv, f_send, f_recv,
    h_sem, r_send, r_recv, z_send, z_recv,
):
    e, t, p = lax.axis_index("expert"), lax.axis_index("tensor"), lax.axis_index("pair")
    z, x_lo = lax.rem(e, NZ), lax.div(e, NZ)
    y, x_hi = lax.div(t, 2), lax.rem(t, 2)
    x = x_hi * 2 + x_lo
    q = x_lo * NT + t
    half = ow.shape[2] * CHUNKS
    width = half // CHUNKS
    ff = wg_hbm.shape[2]
    partner = (e, t, 1 - p)

    def z_peer(j):
        return (x_lo * NZ + lax.rem(z + j, NZ), t, p)

    def plane_peer(j):
        px, py = lax.rem(x + lax.rem(j, 4), 4), lax.rem(y + lax.div(j, 4), 4)
        plo, pt = lax.rem(px, 2), py * 2 + lax.div(px, 2)
        return plo * NT + pt, (plo * NZ + z, pt, p)

    def each(count, fn):
        def step(j, carry):
            fn(j)
            return carry
        lax.fori_loop(1, count, step, 0)

    def remote(src, dst, send, recv, device):
        return pltpu.make_async_remote_copy(
            src_ref=src, dst_ref=dst, send_sem=send, recv_sem=recv,
            device_id=device, device_id_type=MESH,
        )

    def wait_bytes(ref, sem):
        pltpu.make_async_copy(ref, ref, sem).wait()

    barrier = pltpu.get_barrier_semaphore()
    pl.semaphore_signal(barrier, inc=1, device_id=partner, device_id_type=MESH)
    each(NZ, lambda j: pl.semaphore_signal(barrier, inc=1, device_id=z_peer(j), device_id_type=MESH))
    each(NQ, lambda j: pl.semaphore_signal(barrier, inc=1, device_id=plane_peer(j)[1], device_id_type=MESH))

    def mine(index):
        return pl.ds(pl.multiple_of(index * half, half), half)

    loads = [
        pltpu.make_async_copy(ids_hbm, ids, ld.at[0]),
        pltpu.make_async_copy(prob_hbm, prob, ld.at[1]),
        pltpu.make_async_copy(ctx_hbm, ctx, ld.at[2]),
        pltpu.make_async_copy(res_hbm, res, ld.at[3]),
        pltpu.make_async_copy(gain_hbm.at[:, mine(p)], gain, ld.at[4]),
    ]
    ow_loads = [
        pltpu.make_async_copy(ow_hbm.at[:, pl.ds(c * width, width)], ow.at[c], ow_sem.at[c])
        for c in range(CHUNKS)
    ]
    w_loads = []
    for k, side in enumerate((p, 1 - p)):
        w_loads.append(pltpu.make_async_copy(
            wg_hbm.at[0, mine(side), :], wgu.at[k, :, pl.ds(0, ff)], w_sem.at[2 * k]))
        w_loads.append(pltpu.make_async_copy(
            wu_hbm.at[0, mine(side), :], wgu.at[k, :, pl.ds(ff, ff)], w_sem.at[2 * k + 1]))
    wd_load = pltpu.make_async_copy(wd_hbm.at[0, :, mine(p)], wd.at[0], w_sem.at[4])
    for copy in loads[:3] + ow_loads + loads[3:] + w_loads + [wd_load]:
        copy.start()

    loads[0].wait()
    loads[1].wait()
    weights = prob[...] / jnp.sum(prob[...], axis=1, keepdims=True)
    named = ids[...]
    lanes = lax.broadcasted_iota(jnp.int32, (ROWS, 128), 1)
    mark = jnp.zeros((ROWS, 128), F32)
    spread = jnp.zeros((ROWS, 128), F32)
    for k in range(named.shape[1]):
        same = lanes == named[:, k:k + 1]
        mark = jnp.where(same, 1.0, mark)
        spread = jnp.where(same, weights[:, k:k + 1], spread)
    earlier = (
        lax.broadcasted_iota(jnp.int32, (ROWS, ROWS), 1)
        < lax.broadcasted_iota(jnp.int32, (ROWS, ROWS), 0)
    ).astype(F32).astype(BF16)
    code = mark * (1.0 + dot(earlier, mark.astype(BF16)))
    high = spread.astype(BF16)
    meta[0] = code.astype(BF16)
    meta[1] = high
    meta[2] = (spread - high.astype(F32)).astype(BF16)
    metal[:, rows16(z), :] = meta[...]

    loads[2].wait()

    def project(c):
        ow_loads[c].wait()
        attb[c] = dot(ctx[...], ow[c]).astype(BF16)

    def scatter_heads(c):
        def send(j):
            pt = lax.rem(t + j, NT)
            remote(attb.at[c, rows16(pt), :], ars.at[c, rows16(t), :],
                   a_send.at[c], a_recv.at[c], (e, pt, p)).start()
        each(NT, send)

    project(0)
    pl.semaphore_wait(barrier, NZ - 1 + NQ - 1 + 1)
    scatter_heads(0)
    each(NZ, lambda j: remote(meta, metal.at[:, rows16(z), :], m_sem.at[0], m_sem.at[1], z_peer(j)).start())
    for c in range(1, CHUNKS):
        project(c)
        scatter_heads(c)
    wd_swap = remote(wd_hbm.at[0, :, mine(1 - p)], wd.at[1], wd_sem.at[0], wd_sem.at[1], partner)
    wd_swap.start()

    wait_bytes(metal.at[:, pl.ds(0, (NZ - 1) * ROWS), :], m_sem.at[1])
    slots = NQ * ROWS
    tokens = NZ * ROWS

    def expert_of(row):
        place = lax.shift_right_logical(row, 4)
        return (lax.shift_right_logical(place, 3) * (NZ * NT) + z * NT + (place & (NT - 1)))

    pick = (
        lax.broadcasted_iota(jnp.int32, (slots, 128), 1)
        == expert_of(lax.broadcasted_iota(jnp.int32, (slots, 128), 0))
    ).astype(F32).astype(BF16)

    def fits(row, token, codes):
        wanted = ((row & 1) + 1).astype(F32)
        same = (lax.shift_right_logical(row, 1) & (NZ - 1)) == lax.shift_right_logical(token, 4)
        return same & (codes == wanted)

    down_rows = lax.broadcasted_iota(jnp.int32, (slots, tokens), 0)
    down_toks = lax.broadcasted_iota(jnp.int32, (slots, tokens), 1)
    table[...] = jnp.where(fits(down_rows, down_toks, dot_nt(pick, metal[0])), 1.0, 0.0).astype(BF16)
    up_rows = lax.broadcasted_iota(jnp.int32, (tokens, slots), 1)
    up_toks = lax.broadcasted_iota(jnp.int32, (tokens, slots), 0)
    chosen = fits(up_rows, up_toks, dot_nt(metal[0], pick))
    chi[...] = jnp.where(chosen, dot_nt(metal[1], pick), 0.0).astype(BF16)
    clo[...] = jnp.where(chosen, dot_nt(metal[2], pick), 0.0).astype(BF16)

    loads[3].wait()
    loads[4].wait()
    squares = jnp.zeros((ROWS, 1), F32)
    for c in range(CHUNKS):
        ars[c, rows16(t), :] = attb[c, rows16(t), :]
        wait_bytes(ars.at[c, pl.ds(0, (NT - 1) * ROWS), :], a_recv.at[c])
        total = ars[c, 0:ROWS, :].astype(F32)
        for k in range(1, NT):
            total += ars[c, k * ROWS:(k + 1) * ROWS, :].astype(F32)
        part = (res[:, c * width:(c + 1) * width].astype(F32) + total).astype(BF16)
        stream[c] = part
        wide = part.astype(F32)
        squares += jnp.sum(wide * wide, axis=1, keepdims=True)
    ssq[0] = jnp.broadcast_to(squares, (ROWS, 128))
    swap = remote(ssq.at[0], ssq.at[1], s_sem.at[0], s_sem.at[1], partner)
    swap.start()
    swap.wait()
    mean = (ssq[0] + ssq[1])[:, 0:1] * (1.0 / (2 * half))
    scale = lax.rsqrt(mean + EPS)
    for c in range(CHUNKS):
        rows = stream[c].astype(F32) * scale * gain[:, c * width:(c + 1) * width].astype(F32)
        line[c, rows16(z), :] = rows.astype(BF16)
        each(NZ, lambda j: remote(line.at[c, rows16(z), :], line.at[c, rows16(z), :],
                                  g_send.at[c], g_recv.at[c], z_peer(j)).start())

    for copy in w_loads:
        copy.wait()

    def dispatch(c):
        wait_bytes(line.at[c, pl.ds(0, tokens - ROWS), :], g_recv.at[c])
        disp[c] = dot(table[...], line[c]).astype(BF16)

        def send(j):
            pq, device = plane_peer(j)
            remote(disp.at[c, rows16(pq), :], xs.at[0, c, rows16(q), :],
                   d_send.at[c], d_recv.at[c], device).start()
        each(NQ, send)
        xs[0, c, rows16(q), :] = disp[c, rows16(q), :]

    forwards = [
        remote(xs.at[0, c], xs.at[1, c], f_send.at[c], f_recv.at[c], partner) for c in range(CHUNKS)
    ]

    def forward(c):
        wait_bytes(xs.at[0, c, pl.ds(0, slots - ROWS), :], d_recv.at[c])
        forwards[c].start()

    def multiply(c):
        cols = pl.ds(c * width, width)
        own = dot(xs[0, c], wgu[0, cols, :])
        forwards[c].wait_recv()
        both = own + dot(xs[1, c], wgu[1, cols, :])
        if c == 0:
            acc[...] = both
        else:
            acc[...] += both

    for c in range(CHUNKS + 2):
        if c < CHUNKS:
            dispatch(c)
        if 1 <= c <= CHUNKS:
            forward(c - 1)
        if c >= 2:
            multiply(c - 2)

    gate, up = acc[:, 0:ff], acc[:, ff:2 * ff]
    hid[0] = (gate / (1.0 + jnp.exp(-gate)) * up).astype(BF16)
    hid_swap = remote(hid.at[0], hid.at[1], h_sem.at[0], h_sem.at[1], partner)
    hid_swap.start()
    wd_load.wait()
    wd_swap.wait_recv()
    hid_swap.wait_recv()

    def produce(c):
        cols = pl.ds(c * width, width)
        outb[c] = (dot(hid[0], wd[0, :, cols]) + dot(hid[1], wd[1, :, cols])).astype(BF16)

        def send(j):
            pq, device = plane_peer(j)
            remote(outb.at[c, rows16(pq), :], ret.at[c, rows16(q), :],
                   r_send.at[c], r_recv.at[c], device).start()
        each(NQ, send)
        ret[c, rows16(q), :] = outb[c, rows16(q), :]

    def mix(c):
        wait_bytes(ret.at[c, pl.ds(0, slots - ROWS), :], r_recv.at[c])
        mixb[c] = (dot(chi[...], ret[c]) + dot(clo[...], ret[c])).astype(BF16)

        def send(j):
            there = lax.rem(z + j, NZ)
            remote(mixb.at[c, rows16(there), :], zr.at[c, rows16(z), :],
                   z_send.at[c], z_recv.at[c], z_peer(j)).start()
        each(NZ, send)
        zr[c, rows16(z), :] = mixb[c, rows16(z), :]

    def finish(c):
        wait_bytes(zr.at[c, pl.ds(0, tokens - ROWS), :], z_recv.at[c])
        total = stream[c].astype(F32)
        for k in range(NZ):
            total += zr[c, k * ROWS:(k + 1) * ROWS, :].astype(F32)
        out_ref[:, c * width:(c + 1) * width] = total.astype(BF16)

    for c in range(CHUNKS):
        produce(c)
    for c in range(CHUNKS + 1):
        if c < CHUNKS:
            mix(c)
        if c >= 1:
            finish(c - 1)

    wait_bytes(metal.at[:, pl.ds(0, (NZ - 1) * ROWS), :], m_sem.at[0])
    wd_swap.wait_send()
    hid_swap.wait_send()
    for c in range(CHUNKS):
        wait_bytes(ars.at[c, pl.ds(0, (NT - 1) * ROWS), :], a_send.at[c])
        wait_bytes(line.at[c, pl.ds(0, tokens - ROWS), :], g_send.at[c])
        wait_bytes(xs.at[0, c, pl.ds(0, slots - ROWS), :], d_send.at[c])
        forwards[c].wait_send()
        wait_bytes(ret.at[c, pl.ds(0, slots - ROWS), :], r_send.at[c])
        wait_bytes(zr.at[c, pl.ds(0, tokens - ROWS), :], z_send.at[c])


def body(context, out_weight, residual, norm_gain, expert_ids, route_prob, w_gate, w_up, w_down):
    rows, half = residual.shape
    group, depth = context.shape
    ff = w_gate.shape[2]
    width = half // CHUNKS
    slots, tokens = NQ * ROWS, NZ * ROWS
    dma = pltpu.SemaphoreType.DMA
    scratch = [
        pltpu.VMEM((group, depth), BF16),
        pltpu.VMEM((CHUNKS, depth, width), BF16),
        pltpu.VMEM((rows, half), BF16),
        pltpu.VMEM((1, half), BF16),
        pltpu.VMEM(expert_ids.shape, jnp.int32),
        pltpu.VMEM(route_prob.shape, F32),
        pltpu.VMEM((2, half, 2 * ff), BF16),
        pltpu.VMEM((2, ff, half), BF16),
        pltpu.VMEM((CHUNKS, group, width), BF16),
        pltpu.VMEM((CHUNKS, group, width), BF16),
        pltpu.VMEM((CHUNKS, rows, width), BF16),
        pltpu.VMEM((2, rows, 128), F32),
        pltpu.VMEM((3, rows, 128), BF16),
        pltpu.VMEM((3, tokens, 128), BF16),
        pltpu.VMEM((slots, tokens), BF16),
        pltpu.VMEM((tokens, slots), BF16),
        pltpu.VMEM((tokens, slots), BF16),
        pltpu.VMEM((CHUNKS, tokens, width), BF16),
        pltpu.VMEM((CHUNKS, slots, width), BF16),
        pltpu.VMEM((2, CHUNKS, slots, width), BF16),
        pltpu.VMEM((slots, 2 * ff), F32),
        pltpu.VMEM((2, slots, ff), BF16),
        pltpu.VMEM((CHUNKS, slots, width), BF16),
        pltpu.VMEM((CHUNKS, slots, width), BF16),
        pltpu.VMEM((CHUNKS, tokens, width), BF16),
        pltpu.VMEM((CHUNKS, tokens, width), BF16),
        dma((5,)), dma((CHUNKS,)), dma((5,)),
        dma((CHUNKS,)), dma((CHUNKS,)), dma((2,)), dma((2,)), dma((2,)),
        dma((CHUNKS,)), dma((CHUNKS,)), dma((CHUNKS,)), dma((CHUNKS,)),
        dma((CHUNKS,)), dma((CHUNKS,)),
        dma((2,)), dma((CHUNKS,)), dma((CHUNKS,)), dma((CHUNKS,)), dma((CHUNKS,)),
    ]
    return pl.pallas_call(
        kernel,
        out_shape=jax.ShapeDtypeStruct((rows, half), BF16),
        in_specs=[pl.BlockSpec(memory_space=pl.ANY)] * 9,
        out_specs=pl.BlockSpec(memory_space=pltpu.VMEM),
        scratch_shapes=scratch,
        compiler_params=pltpu.CompilerParams(
            collective_id=0, has_side_effects=True, vmem_limit_bytes=48 * 1024 * 1024
        ),
        name="block",
    )(
        context, out_weight, residual, norm_gain.reshape(1, -1), expert_ids, route_prob,
        w_gate, w_up, w_down,
    )


def solution(mesh):
    placed = (
        P("expert", "tensor"),
        P("tensor", "pair"),
        P(("expert", "tensor"), "pair"),
        P(),
        P(("expert", "tensor"), None),
        P(("expert", "tensor"), None),
        P(("expert", "tensor"), None, "pair"),
        P(("expert", "tensor"), None, "pair"),
        P(("expert", "tensor"), "pair", None),
    )
    return jax.shard_map(
        body, mesh=mesh, in_specs=placed, out_specs=P(("expert", "tensor"), "pair"), check_vma=False
    )
```

```python
import functools

import jax
import jax.numpy as jnp
from jax import lax
from jax.experimental import pallas as pl
from jax.experimental.pallas import tpu as pltpu
from jax.sharding import PartitionSpec as P

EPS = 1e-06
MESH = pl.DeviceIdType.MESH
BF16 = jnp.bfloat16
F32 = jnp.float32
ROWS = 16
NZ = 8
NT = 8
NQ = 16
WIDTHS = (512, 512, 512, 512)
CHUNKS = len(WIDTHS)
STARTS = tuple(sum(WIDTHS[:c]) for c in range(CHUNKS))
AHEAD = 3
WAY_OUT = ("T0", "G0", "S3", "G1", "D0", "G2", "U0", "D1", "G3", "F0", "D2", "F1", "M0", "D3", "F2", "M1", "F3", "M2", "M3")
WAY_BACK = ("P0", "P1", "P2", "X0", "P3", "X1", "X2", "E0", "X3", "E1", "E2", "E3")
EXTRA = 128


def dot(a, b):
    return jnp.dot(a, b, preferred_element_type=F32)


def dot_nt(a, b):
    return lax.dot_general(a, b, (((1,), (1,)), ((), ())), preferred_element_type=F32)


def rows16(index):
    return pl.ds(pl.multiple_of(index * ROWS, ROWS), ROWS)


def kernel(
    ctx_hbm, ow_hbm, res_hbm, gain_hbm, ids_hbm, prob_hbm, wg_hbm, wu_hbm, wd_hbm, out_ref,
    ctx, ow, res, gain, ids, prob, wgu, wd,
    attb, ars, stream, meta, metal, table, chi, clo,
    line, disp, xs, acc, hid, outb, ret, mixb, zr,
    ld, ow_sem, w_sem,
    a_send, a_recv, m_sem, wd_sem, g_send, g_recv, d_send, d_recv, f_send, f_recv,
    h_sem, r_send, r_recv, z_send, z_recv,
):
    e, t, p = lax.axis_index("expert"), lax.axis_index("tensor"), lax.axis_index("pair")
    z, x_lo = lax.rem(e, NZ), lax.div(e, NZ)
    y, x_hi = lax.div(t, 2), lax.rem(t, 2)
    x = x_hi * 2 + x_lo
    q = x_lo * NT + t
    half = ow.shape[1]
    ff = wg_hbm.shape[2]
    slots = NQ * ROWS
    tokens = NZ * ROWS
    partner = (e, t, 1 - p)

    def along(j):
        return lax.rem(z + j, NZ)

    def z_peer(j):
        return (x_lo * NZ + along(j), t, p)

    def plane_peer(j):
        px, py = lax.rem(x + lax.rem(j, 4), 4), lax.rem(y + lax.div(j, 4), 4)
        plo, pt = lax.rem(px, 2), py * 2 + lax.div(px, 2)
        return plo * NT + pt, (plo * NZ + z, pt, p)

    def each(count, fn):
        def step(j, carry):
            fn(j)
            return carry
        lax.fori_loop(1, count, step, 0)

    def remote(src, dst, send, recv, device):
        return pltpu.make_async_remote_copy(
            src_ref=src, dst_ref=dst, send_sem=send, recv_sem=recv,
            device_id=device, device_id_type=MESH,
        )

    def wait_bytes(ref, sem):
        pltpu.make_async_copy(ref, ref, sem).wait()

    def cols(c):
        return pl.ds(STARTS[c], WIDTHS[c])

    def more(c):
        return pl.ds(STARTS[c], WIDTHS[c] + (EXTRA if c == CHUNKS - 1 else 0))

    def mine(index):
        return pl.ds(pl.multiple_of(index * half, half), half)

    pending = []

    loads = [
        pltpu.make_async_copy(ctx_hbm, ctx, ld.at[0]),
        pltpu.make_async_copy(res_hbm, res, ld.at[1]),
        pltpu.make_async_copy(gain_hbm.at[mine(p)], gain, ld.at[2]),
        pltpu.make_async_copy(ids_hbm, ids, ld.at[3]),
        pltpu.make_async_copy(prob_hbm, prob, ld.at[4]),
    ]
    ow_loads = [
        pltpu.make_async_copy(ow_hbm.at[:, cols(c)], ow.at[:, cols(c)], ow_sem.at[c])
        for c in range(CHUNKS)
    ]
    w_loads = []
    for k, side in enumerate((p, 1 - p)):
        w_loads.append(pltpu.make_async_copy(
            wg_hbm.at[0, mine(side), :], wgu.at[k, :, pl.ds(0, ff)], w_sem.at[2 * k]))
        w_loads.append(pltpu.make_async_copy(
            wu_hbm.at[0, mine(side), :], wgu.at[k, :, pl.ds(ff, ff)], w_sem.at[2 * k + 1]))
    wd_load = pltpu.make_async_copy(wd_hbm.at[0, :, mine(p)], wd.at[0], w_sem.at[4])
    for copy in loads[:1] + ow_loads + loads[1:]:
        copy.start()

    barrier = pltpu.get_barrier_semaphore()
    each(NQ, lambda j: pl.semaphore_signal(barrier, inc=1, device_id=plane_peer(j)[1], device_id_type=MESH))
    each(NZ, lambda j: pl.semaphore_signal(barrier, inc=1, device_id=z_peer(j), device_id_type=MESH))
    pl.semaphore_signal(barrier, inc=1, device_id=partner, device_id_type=MESH)

    def project(c):
        ow_loads[c].wait()
        attb[:, cols(c)] = dot(ctx[...], ow[:, cols(c)]).astype(BF16)

    def scatter_heads(c):
        def send(j):
            pt = lax.rem(t + j, NT)
            remote(attb.at[rows16(pt), cols(c)], ars.at[rows16(t), cols(c)],
                   a_send.at[c], a_recv.at[c], (e, pt, p)).start()
        each(NT, send)
        pending.append(lambda: wait_bytes(ars.at[pl.ds(0, (NT - 1) * ROWS), cols(c)], a_send.at[c]))

    loads[0].wait()
    project(0)
    pl.semaphore_wait(barrier, NZ - 1 + NQ - 1 + 1)
    scatter_heads(0)
    for c in range(1, AHEAD):
        project(c)
        scatter_heads(c)
    for copy in w_loads + [wd_load]:
        copy.start()

    for copy in loads[1:]:
        copy.wait()
    weights = prob[...] / jnp.sum(prob[...], axis=0, keepdims=True)
    named = ids[...]
    experts = lax.broadcasted_iota(jnp.int32, (128, ROWS), 0)
    mark = jnp.zeros((128, ROWS), F32)
    spread = jnp.zeros((128, ROWS), F32)
    for k in range(named.shape[0]):
        same = experts == named[k:k + 1, :]
        mark = jnp.where(same, 1.0, mark)
        spread = jnp.where(same, weights[k:k + 1, :], spread)
    before = lax.broadcasted_iota(jnp.int32, (ROWS, ROWS), 1)
    after = lax.broadcasted_iota(jnp.int32, (ROWS, ROWS), 0)
    earlier = (before < after).astype(F32).astype(BF16)
    same_row = (before == after).astype(F32).astype(BF16)
    mark = mark.astype(BF16)
    high = spread.astype(BF16)
    low = (spread - high.astype(F32)).astype(BF16)
    meta[0] = (dot_nt(same_row, mark) * (1.0 + dot_nt(earlier, mark))).astype(BF16)
    meta[1] = dot_nt(same_row, high).astype(BF16)
    meta[2] = dot_nt(same_row, low).astype(BF16)
    metal[:, rows16(z), :] = meta[...]
    each(NZ, lambda j: remote(meta, metal.at[:, rows16(z), :], m_sem.at[0], m_sem.at[1], z_peer(j)).start())
    pending.append(lambda: wait_bytes(metal.at[:, pl.ds(0, (NZ - 1) * ROWS), :], m_sem.at[0]))
    wd_swap = remote(wd_hbm.at[0, :, mine(1 - p)], wd.at[1], wd_sem.at[0], wd_sem.at[1], partner)
    wd_swap.start()
    pending.append(wd_swap.wait_send)

    def expert_of(row):
        place = lax.shift_right_logical(row, 4)
        return (lax.shift_right_logical(place, 3) * (NZ * NT) + z * NT + (place & (NT - 1)))

    def fits(row, token, codes):
        wanted = ((row & 1) + 1).astype(F32)
        same = (lax.shift_right_logical(row, 1) & (NZ - 1)) == lax.shift_right_logical(token, 4)
        return same & (codes == wanted)

    def iota(rows, columns, axis):
        return lax.broadcasted_iota(jnp.int32, (rows, columns), axis)

    def picker():
        return (iota(slots, 128, 1) == expert_of(iota(slots, 128, 0))).astype(F32).astype(BF16)

    def down_table():
        wait_bytes(metal.at[:, pl.ds(0, (NZ - 1) * ROWS), :], m_sem.at[1])
        codes = dot_nt(picker(), metal[0])
        chosen = fits(iota(slots, tokens, 0), iota(slots, tokens, 1), codes)
        table[...] = jnp.where(chosen, 1.0, 0.0).astype(BF16)

    def up_tables():
        pick = picker()
        chosen = fits(iota(tokens, slots, 1), iota(tokens, slots, 0), dot_nt(metal[0], pick))
        chi[...] = jnp.where(chosen, dot_nt(metal[1], pick), 0.0).astype(BF16)
        clo[...] = jnp.where(chosen, dot_nt(metal[2], pick), 0.0).astype(BF16)

    squares = [jnp.zeros((ROWS, 1), F32)]

    def gather_heads(c):
        ars[rows16(t), cols(c)] = attb[rows16(t), cols(c)]
        wait_bytes(ars.at[pl.ds(0, (NT - 1) * ROWS), cols(c)], a_recv.at[c])
        total = res[:, cols(c)].astype(F32)
        heads = ars[0:ROWS, cols(c)].astype(F32)
        for k in range(1, NT):
            heads += ars[k * ROWS:(k + 1) * ROWS, cols(c)].astype(F32)
        part = (total + heads).astype(BF16)
        stream[:, cols(c)] = part
        wide = part.astype(F32)
        squares[0] = squares[0] + jnp.sum(wide * wide, axis=1, keepdims=True)
        line[rows16(z), cols(c)] = (wide * gain[cols(c)].astype(F32)[None, :]).astype(BF16)
        if c == CHUNKS - 1:
            top = squares[0].astype(BF16).astype(F32)
            middle = (squares[0] - top).astype(BF16).astype(F32)
            lane = iota(ROWS, EXTRA, 1)
            parts = jnp.where(lane == 0, top, jnp.where(lane == 1, middle, squares[0] - top - middle))
            line[rows16(z), pl.ds(half, EXTRA)] = jnp.where(lane < 3, parts, 0.0).astype(BF16)
        each(NZ, lambda j: remote(line.at[rows16(z), more(c)], line.at[rows16(z), more(c)],
                                  g_send.at[c], g_recv.at[c], z_peer(j)).start())
        pending.append(lambda: wait_bytes(line.at[pl.ds(0, tokens - ROWS), more(c)], g_send.at[c]))

    def dispatch(c):
        wait_bytes(line.at[pl.ds(0, tokens - ROWS), more(c)], g_recv.at[c])
        disp[:, more(c)] = dot(table[...], line[:, more(c)]).astype(BF16)

        def send(j):
            pq, device = plane_peer(j)
            remote(disp.at[rows16(pq), more(c)], xs.at[0, rows16(q), more(c)],
                   d_send.at[c], d_recv.at[c], device).start()
        each(NQ, send)
        pending.append(lambda: wait_bytes(xs.at[0, pl.ds(0, slots - ROWS), more(c)], d_send.at[c]))
        xs[0, rows16(q), more(c)] = disp[rows16(q), more(c)]

    forwards = [
        remote(xs.at[0, :, more(c)], xs.at[1, :, more(c)], f_send.at[c], f_recv.at[c], partner)
        for c in range(CHUNKS)
    ]

    def forward(c):
        wait_bytes(xs.at[0, pl.ds(0, slots - ROWS), more(c)], d_recv.at[c])
        forwards[c].start()
        pending.append(forwards[c].wait_send)

    def multiply(c):
        own = dot(xs[0, :, cols(c)], wgu[0, cols(c), :])
        forwards[c].wait_recv()
        both = own + dot(xs[1, :, cols(c)], wgu[1, cols(c), :])
        if c == 0:
            acc[...] = both
        else:
            acc[...] += both

    def head_start(c):
        project(c)
        scatter_heads(c)

    def tables():
        up_tables()
        for copy in w_loads:
            copy.wait()

    steps = {
        "S": head_start, "G": gather_heads, "D": dispatch, "F": forward, "M": multiply,
        "T": lambda c: down_table(), "U": lambda c: tables(),
    }
    for name in WAY_OUT:
        steps[name[0]](int(name[1]))

    sums = jnp.sum(xs[0, :, pl.ds(half, EXTRA)].astype(F32) + xs[1, :, pl.ds(half, EXTRA)].astype(F32),
                   axis=1, keepdims=True)
    scale = lax.rsqrt(sums * (1.0 / (2 * half)) + EPS)
    gate, up = acc[:, 0:ff] * scale, acc[:, ff:2 * ff] * scale
    hid[0] = (gate / (1.0 + jnp.exp(-gate)) * up).astype(BF16)
    hid_swap = remote(hid.at[0], hid.at[1], h_sem.at[0], h_sem.at[1], partner)
    hid_swap.start()
    pending.append(hid_swap.wait_send)
    wd_load.wait()
    wd_swap.wait_recv()
    hid_swap.wait_recv()

    def produce(c):
        outb[:, cols(c)] = (dot(hid[0], wd[0, :, cols(c)]) + dot(hid[1], wd[1, :, cols(c)])).astype(BF16)

        def send(j):
            pq, device = plane_peer(j)
            remote(outb.at[rows16(pq), cols(c)], ret.at[rows16(q), cols(c)],
                   r_send.at[c], r_recv.at[c], device).start()
        each(NQ, send)
        pending.append(lambda: wait_bytes(ret.at[pl.ds(0, slots - ROWS), cols(c)], r_send.at[c]))
        ret[rows16(q), cols(c)] = outb[rows16(q), cols(c)]

    def mix(c):
        wait_bytes(ret.at[pl.ds(0, slots - ROWS), cols(c)], r_recv.at[c])
        mixb[:, cols(c)] = (dot(chi[...], ret[:, cols(c)]) + dot(clo[...], ret[:, cols(c)])).astype(BF16)

        def send(j):
            remote(mixb.at[rows16(along(j)), cols(c)], zr.at[rows16(z), cols(c)],
                   z_send.at[c], z_recv.at[c], z_peer(j)).start()
        each(NZ, send)
        pending.append(lambda: wait_bytes(zr.at[pl.ds(0, tokens - ROWS), cols(c)], z_send.at[c]))
        zr[rows16(z), cols(c)] = mixb[rows16(z), cols(c)]

    def finish(c):
        wait_bytes(zr.at[pl.ds(0, tokens - ROWS), cols(c)], z_recv.at[c])
        total = stream[:, cols(c)].astype(F32)
        for k in range(NZ):
            total += zr[k * ROWS:(k + 1) * ROWS, cols(c)].astype(F32)
        out_ref[:, cols(c)] = total.astype(BF16)

    steps = {"P": produce, "X": mix, "E": finish}
    for name in WAY_BACK:
        steps[name[0]](int(name[1]))

    for wait in pending:
        wait()


def body(context, out_weight, residual, norm_gain, expert_ids, route_prob, w_gate, w_up, w_down):
    rows, half = residual.shape
    group, depth = context.shape
    ff = w_gate.shape[2]
    slots, tokens = NQ * ROWS, NZ * ROWS
    dma = pltpu.SemaphoreType.DMA
    scratch = [
        pltpu.VMEM((group, depth), BF16),
        pltpu.VMEM((depth, half), BF16),
        pltpu.VMEM((rows, half), BF16),
        pltpu.VMEM((half,), BF16),
        pltpu.VMEM(expert_ids.shape[::-1], jnp.int32),
        pltpu.VMEM(route_prob.shape[::-1], F32),
        pltpu.VMEM((2, half, 2 * ff), BF16),
        pltpu.VMEM((2, ff, half), BF16),
        pltpu.VMEM((group, half), BF16),
        pltpu.VMEM((group, half), BF16),
        pltpu.VMEM((rows, half), BF16),
        pltpu.VMEM((3, rows, 128), BF16),
        pltpu.VMEM((3, tokens, 128), BF16),
        pltpu.VMEM((slots, tokens), BF16),
        pltpu.VMEM((tokens, slots), BF16),
        pltpu.VMEM((tokens, slots), BF16),
        pltpu.VMEM((tokens, half + EXTRA), BF16),
        pltpu.VMEM((slots, half + EXTRA), BF16),
        pltpu.VMEM((2, slots, half + EXTRA), BF16),
        pltpu.VMEM((slots, 2 * ff), F32),
        pltpu.VMEM((2, slots, ff), BF16),
        pltpu.VMEM((slots, half), BF16),
        pltpu.VMEM((slots, half), BF16),
        pltpu.VMEM((tokens, half), BF16),
        pltpu.VMEM((tokens, half), BF16),
        dma((5,)), dma((CHUNKS,)), dma((5,)),
        dma((CHUNKS,)), dma((CHUNKS,)), dma((2,)), dma((2,)),
        dma((CHUNKS,)), dma((CHUNKS,)), dma((CHUNKS,)), dma((CHUNKS,)),
        dma((CHUNKS,)), dma((CHUNKS,)),
        dma((2,)), dma((CHUNKS,)), dma((CHUNKS,)), dma((CHUNKS,)), dma((CHUNKS,)),
    ]
    return pl.pallas_call(
        kernel,
        out_shape=jax.ShapeDtypeStruct((rows, half), BF16),
        in_specs=[pl.BlockSpec(memory_space=pltpu.HBM)] * 9,
        out_specs=pl.BlockSpec(memory_space=pltpu.VMEM),
        scratch_shapes=scratch,
        compiler_params=pltpu.CompilerParams(
            collective_id=0, has_side_effects=True, vmem_limit_bytes=60 * 1024 * 1024
        ),
        name="block",
    )(
        context, out_weight, residual, norm_gain, expert_ids.T, route_prob.T,
        w_gate, w_up, w_down,
    )


def solution(mesh):
    placed = (
        P("expert", "tensor"),
        P("tensor", "pair"),
        P(("expert", "tensor"), "pair"),
        P(),
        P(("expert", "tensor"), None),
        P(("expert", "tensor"), None),
        P(("expert", "tensor"), None, "pair"),
        P(("expert", "tensor"), None, "pair"),
        P(("expert", "tensor"), "pair", None),
    )
    return jax.shard_map(
        body, mesh=mesh, in_specs=placed, out_specs=P(("expert", "tensor"), "pair"), check_vma=False
    )
```

```python
import functools

import jax
import jax.numpy as jnp
from jax import lax
from jax.experimental import pallas as pl
from jax.experimental.pallas import tpu as pltpu
from jax.sharding import PartitionSpec as P

EPS = 1e-06
MESH = pl.DeviceIdType.MESH
BF16 = jnp.bfloat16
F32 = jnp.float32
ROWS = 16
NZ = 8
NT = 8
NQ = 16
WIDTHS = (512, 512, 512, 512)
CHUNKS = len(WIDTHS)
STARTS = tuple(sum(WIDTHS[:c]) for c in range(CHUNKS))
AHEAD = 2
WAY_OUT = ("T0", "G0", "S2", "G1", "S3", "D0", "G2", "D1", "G3", "F0", "D2", "U0", "F1", "D3", "M0", "F2", "M1", "F3", "M2", "M3")
WAY_BACK = ("P0", "P1", "P2", "X0", "P3", "Q0", "X1", "X2", "E0", "X3", "E1", "E2", "E3")
EXTRA = 128


def dot(a, b):
    return jnp.dot(a, b, preferred_element_type=F32)


def dot_nt(a, b):
    return lax.dot_general(a, b, (((1,), (1,)), ((), ())), preferred_element_type=F32)


def rows16(index):
    return pl.ds(pl.multiple_of(index * ROWS, ROWS), ROWS)


def kernel(
    ctx_hbm, ow_hbm, res_hbm, gain_hbm, ids_hbm, prob_hbm, wg_hbm, wu_hbm, wd_hbm, out_ref,
    ctx, ow, res, gain, ids, prob, wgu, wd,
    attb, ars, stream, meta, metal, table, chi, clo,
    line, disp, xs, acc, hid, outb, ret, mixb, zr,
    ld, ow_sem, w_sem,
    a_send, a_recv, m_sem, wd_sem, g_send, g_recv, d_send, d_recv, f_send, f_recv,
    h_sem, r_send, r_recv, z_send, z_recv, o_sem, result,
):
    e, t, p = lax.axis_index("expert"), lax.axis_index("tensor"), lax.axis_index("pair")
    z, x_lo = lax.rem(e, NZ), lax.div(e, NZ)
    y, x_hi = lax.div(t, 2), lax.rem(t, 2)
    x = x_hi * 2 + x_lo
    q = x_lo * NT + t
    half = ow.shape[1]
    ff = wg_hbm.shape[2]
    slots = NQ * ROWS
    tokens = NZ * ROWS
    partner = (e, t, 1 - p)

    def along(j):
        return lax.rem(z + j, NZ)

    def z_peer(j):
        return (x_lo * NZ + along(j), t, p)

    def plane_peer(j):
        px, py = lax.rem(x + lax.rem(j, 4), 4), lax.rem(y + lax.div(j, 4), 4)
        plo, pt = lax.rem(px, 2), py * 2 + lax.div(px, 2)
        return plo * NT + pt, (plo * NZ + z, pt, p)

    def each(count, fn):
        def step(j, carry):
            fn(j)
            return carry
        lax.fori_loop(1, count, step, 0)

    def remote(src, dst, send, recv, device):
        return pltpu.make_async_remote_copy(
            src_ref=src, dst_ref=dst, send_sem=send, recv_sem=recv,
            device_id=device, device_id_type=MESH,
        )

    def wait_bytes(ref, sem):
        pltpu.make_async_copy(ref, ref, sem).wait()

    def cols(c):
        return pl.ds(STARTS[c], WIDTHS[c])

    def more(c):
        return pl.ds(STARTS[c], WIDTHS[c] + (EXTRA if c == CHUNKS - 1 else 0))

    def mine(index):
        return pl.ds(pl.multiple_of(index * half, half), half)

    pending = []

    def drain(count):
        for _ in range(count):
            pending.pop(0)()

    loads = [
        pltpu.make_async_copy(ctx_hbm, ctx, ld.at[0]),
        pltpu.make_async_copy(res_hbm, res, ld.at[1]),
        pltpu.make_async_copy(gain_hbm.at[mine(p)], gain, ld.at[2]),
        pltpu.make_async_copy(ids_hbm, ids, ld.at[3]),
        pltpu.make_async_copy(prob_hbm, prob, ld.at[4]),
    ]
    ow_loads = [
        pltpu.make_async_copy(ow_hbm.at[:, cols(c)], ow.at[:, cols(c)], ow_sem.at[c])
        for c in range(CHUNKS)
    ]
    w_loads = []
    for k, side in enumerate((p, 1 - p)):
        w_loads.append(pltpu.make_async_copy(
            wg_hbm.at[0, mine(side), :], wgu.at[k, :, pl.ds(0, ff)], w_sem.at[2 * k]))
        w_loads.append(pltpu.make_async_copy(
            wu_hbm.at[0, mine(side), :], wgu.at[k, :, pl.ds(ff, ff)], w_sem.at[2 * k + 1]))
    wd_load = pltpu.make_async_copy(wd_hbm.at[0, :, mine(p)], wd.at[pl.ds(0, ff), :], w_sem.at[4])
    for copy in loads[:1] + ow_loads + loads[1:]:
        copy.start()

    barrier = pltpu.get_barrier_semaphore()
    each(NQ, lambda j: pl.semaphore_signal(barrier, inc=1, device_id=plane_peer(j)[1], device_id_type=MESH))
    each(NZ, lambda j: pl.semaphore_signal(barrier, inc=1, device_id=z_peer(j), device_id_type=MESH))
    pl.semaphore_signal(barrier, inc=1, device_id=partner, device_id_type=MESH)

    def project(c):
        ow_loads[c].wait()
        attb[:, cols(c)] = dot(ctx[...], ow[:, cols(c)]).astype(BF16)

    def scatter_heads(c):
        def send(j):
            pt = lax.rem(t + j, NT)
            remote(attb.at[rows16(pt), cols(c)], ars.at[rows16(t), cols(c)],
                   a_send.at[c], a_recv.at[c], (e, pt, p)).start()
        each(NT, send)
        pending.append(lambda: wait_bytes(ars.at[pl.ds(0, (NT - 1) * ROWS), cols(c)], a_send.at[c]))

    loads[0].wait()
    project(0)
    pl.semaphore_wait(barrier, NZ - 1 + NQ - 1 + 1)
    scatter_heads(0)
    for c in range(1, AHEAD):
        project(c)
        scatter_heads(c)
    for copy in w_loads + [wd_load]:
        copy.start()

    for copy in loads[1:]:
        copy.wait()
    weights = prob[...] / jnp.sum(prob[...], axis=0, keepdims=True)
    named = ids[...]
    experts = lax.broadcasted_iota(jnp.int32, (128, ROWS), 0)
    mark = jnp.zeros((128, ROWS), F32)
    spread = jnp.zeros((128, ROWS), F32)
    for k in range(named.shape[0]):
        same = experts == named[k:k + 1, :]
        mark = jnp.where(same, 1.0, mark)
        spread = jnp.where(same, weights[k:k + 1, :], spread)
    before = lax.broadcasted_iota(jnp.int32, (ROWS, ROWS), 1)
    after = lax.broadcasted_iota(jnp.int32, (ROWS, ROWS), 0)
    earlier = (before < after).astype(F32).astype(BF16)
    same_row = (before == after).astype(F32).astype(BF16)
    mark = mark.astype(BF16)
    high = spread.astype(BF16)
    low = (spread - high.astype(F32)).astype(BF16)
    meta[0] = (dot_nt(same_row, mark) * (1.0 + dot_nt(earlier, mark))).astype(BF16)
    meta[1] = dot_nt(same_row, high).astype(BF16)
    meta[2] = dot_nt(same_row, low).astype(BF16)
    metal[:, rows16(z), :] = meta[...]
    each(NZ, lambda j: remote(meta, metal.at[:, rows16(z), :], m_sem.at[0], m_sem.at[1], z_peer(j)).start())
    pending.append(lambda: wait_bytes(metal.at[:, pl.ds(0, (NZ - 1) * ROWS), :], m_sem.at[0]))
    wd_swap = remote(wd_hbm.at[0, :, mine(1 - p)], wd.at[pl.ds(ff, ff), :], wd_sem.at[0], wd_sem.at[1], partner)
    wd_swap.start()
    pending.append(wd_swap.wait_send)

    def expert_of(row):
        place = lax.shift_right_logical(row, 4)
        return (lax.shift_right_logical(place, 3) * (NZ * NT) + z * NT + (place & (NT - 1)))

    def fits(row, token, codes):
        wanted = ((row & 1) + 1).astype(F32)
        same = (lax.shift_right_logical(row, 1) & (NZ - 1)) == lax.shift_right_logical(token, 4)
        return same & (codes == wanted)

    def iota(rows, columns, axis):
        return lax.broadcasted_iota(jnp.int32, (rows, columns), axis)

    def picker():
        return (iota(slots, 128, 1) == expert_of(iota(slots, 128, 0))).astype(F32).astype(BF16)

    def down_table():
        wait_bytes(metal.at[:, pl.ds(0, (NZ - 1) * ROWS), :], m_sem.at[1])
        codes = dot_nt(picker(), metal[0])
        chosen = fits(iota(slots, tokens, 0), iota(slots, tokens, 1), codes)
        table[...] = jnp.where(chosen, 1.0, 0.0).astype(BF16)

    def up_tables():
        pick = picker()
        chosen = fits(iota(tokens, slots, 1), iota(tokens, slots, 0), dot_nt(metal[0], pick))
        chi[...] = jnp.where(chosen, dot_nt(metal[1], pick), 0.0).astype(BF16)
        clo[...] = jnp.where(chosen, dot_nt(metal[2], pick), 0.0).astype(BF16)

    squares = [jnp.zeros((ROWS, 1), F32)]

    def gather_heads(c):
        ars[rows16(t), cols(c)] = attb[rows16(t), cols(c)]
        wait_bytes(ars.at[pl.ds(0, (NT - 1) * ROWS), cols(c)], a_recv.at[c])
        total = res[:, cols(c)].astype(F32)
        heads = ars[0:ROWS, cols(c)].astype(F32)
        for k in range(1, NT):
            heads += ars[k * ROWS:(k + 1) * ROWS, cols(c)].astype(F32)
        part = (total + heads).astype(BF16)
        stream[:, cols(c)] = part
        wide = part.astype(F32)
        squares[0] = squares[0] + jnp.sum(wide * wide, axis=1, keepdims=True)
        line[rows16(z), cols(c)] = (wide * gain[cols(c)].astype(F32)[None, :]).astype(BF16)
        if c == CHUNKS - 1:
            top = squares[0].astype(BF16).astype(F32)
            middle = (squares[0] - top).astype(BF16).astype(F32)
            lane = iota(ROWS, EXTRA, 1)
            parts = jnp.where(lane == 0, top, jnp.where(lane == 1, middle, squares[0] - top - middle))
            line[rows16(z), pl.ds(half, EXTRA)] = jnp.where(lane < 3, parts, 0.0).astype(BF16)
        each(NZ, lambda j: remote(line.at[rows16(z), more(c)], line.at[rows16(z), more(c)],
                                  g_send.at[c], g_recv.at[c], z_peer(j)).start())
        pending.append(lambda: wait_bytes(line.at[pl.ds(0, tokens - ROWS), more(c)], g_send.at[c]))

    def dispatch(c):
        wait_bytes(line.at[pl.ds(0, tokens - ROWS), more(c)], g_recv.at[c])
        disp[:, more(c)] = dot(table[...], line[:, more(c)]).astype(BF16)

        def send(j):
            pq, device = plane_peer(j)
            remote(disp.at[rows16(pq), more(c)], xs.at[0, rows16(q), more(c)],
                   d_send.at[c], d_recv.at[c], device).start()
        each(NQ, send)
        pending.append(lambda: wait_bytes(xs.at[0, pl.ds(0, slots - ROWS), more(c)], d_send.at[c]))
        xs[0, rows16(q), more(c)] = disp[rows16(q), more(c)]

    forwards = [
        remote(xs.at[0, :, more(c)], xs.at[1, :, more(c)], f_send.at[c], f_recv.at[c], partner)
        for c in range(CHUNKS)
    ]

    def forward(c):
        wait_bytes(xs.at[0, pl.ds(0, slots - ROWS), more(c)], d_recv.at[c])
        forwards[c].start()
        pending.append(forwards[c].wait_send)

    def multiply(c):
        own = dot(xs[0, :, cols(c)], wgu[0, cols(c), :])
        forwards[c].wait_recv()
        both = own + dot(xs[1, :, cols(c)], wgu[1, cols(c), :])
        if c == 0:
            acc[...] = both
        else:
            acc[...] += both

    def head_start(c):
        project(c)
        scatter_heads(c)

    def tables():
        up_tables()
        for copy in w_loads:
            copy.wait()

    steps = {
        "S": head_start, "G": gather_heads, "D": dispatch, "F": forward, "M": multiply,
        "T": lambda c: down_table(), "U": lambda c: tables(),
    }
    for name in WAY_OUT:
        steps[name[0]](int(name[1]))

    sums = jnp.sum(xs[0, :, pl.ds(half, EXTRA)].astype(F32) + xs[1, :, pl.ds(half, EXTRA)].astype(F32),
                   axis=1, keepdims=True)
    scale = lax.rsqrt(sums * (1.0 / (2 * half)) + EPS)
    gate, up = acc[:, 0:ff] * scale, acc[:, ff:2 * ff] * scale
    hid[:, 0:ff] = (gate / (1.0 + jnp.exp(-gate)) * up).astype(BF16)
    hid_swap = remote(hid.at[:, pl.ds(0, ff)], hid.at[:, pl.ds(ff, ff)], h_sem.at[0], h_sem.at[1], partner)
    hid_swap.start()
    pending.append(hid_swap.wait_send)
    wd_load.wait()
    wd_swap.wait_recv()
    hid_swap.wait_recv()
    early = len(pending)

    def produce(c):
        outb[:, cols(c)] = dot(hid[...], wd[:, cols(c)]).astype(BF16)

        def send(j):
            pq, device = plane_peer(j)
            remote(outb.at[rows16(pq), cols(c)], ret.at[rows16(q), cols(c)],
                   r_send.at[c], r_recv.at[c], device).start()
        each(NQ, send)
        pending.append(lambda: wait_bytes(ret.at[pl.ds(0, slots - ROWS), cols(c)], r_send.at[c]))
        ret[rows16(q), cols(c)] = outb[rows16(q), cols(c)]

    def mix(c):
        wait_bytes(ret.at[pl.ds(0, slots - ROWS), cols(c)], r_recv.at[c])
        mixb[:, cols(c)] = (dot(chi[...], ret[:, cols(c)]) + dot(clo[...], ret[:, cols(c)])).astype(BF16)

        def send(j):
            remote(mixb.at[rows16(along(j)), cols(c)], zr.at[rows16(z), cols(c)],
                   z_send.at[c], z_recv.at[c], z_peer(j)).start()
        each(NZ, send)
        pending.append(lambda: wait_bytes(zr.at[pl.ds(0, tokens - ROWS), cols(c)], z_send.at[c]))
        zr[rows16(z), cols(c)] = mixb[rows16(z), cols(c)]

    def finish(c):
        wait_bytes(zr.at[pl.ds(0, tokens - ROWS), cols(c)], z_recv.at[c])
        total = stream[:, cols(c)].astype(F32)
        for k in range(NZ):
            total += zr[k * ROWS:(k + 1) * ROWS, cols(c)].astype(F32)
        result[:, cols(c)] = total.astype(BF16)
        leave = pltpu.make_async_copy(result.at[:, cols(c)], out_ref.at[:, cols(c)], o_sem.at[c])
        leave.start()
        pending.append(leave.wait)

    steps = {"P": produce, "X": mix, "E": finish, "Q": lambda c: drain(early if c == 0 else CHUNKS)}
    for name in WAY_BACK:
        steps[name[0]](int(name[1]))

    drain(len(pending))


def body(context, out_weight, residual, norm_gain, expert_ids, route_prob, w_gate, w_up, w_down):
    rows, half = residual.shape
    group, depth = context.shape
    ff = w_gate.shape[2]
    slots, tokens = NQ * ROWS, NZ * ROWS
    dma = pltpu.SemaphoreType.DMA
    scratch = [
        pltpu.VMEM((group, depth), BF16),
        pltpu.VMEM((depth, half), BF16),
        pltpu.VMEM((rows, half), BF16),
        pltpu.VMEM((half,), BF16),
        pltpu.VMEM(expert_ids.shape[::-1], jnp.int32),
        pltpu.VMEM(route_prob.shape[::-1], F32),
        pltpu.VMEM((2, half, 2 * ff), BF16),
        pltpu.VMEM((2 * ff, half), BF16),
        pltpu.VMEM((group, half), BF16),
        pltpu.VMEM((group, half), BF16),
        pltpu.VMEM((rows, half), BF16),
        pltpu.VMEM((3, rows, 128), BF16),
        pltpu.VMEM((3, tokens, 128), BF16),
        pltpu.VMEM((slots, tokens), BF16),
        pltpu.VMEM((tokens, slots), BF16),
        pltpu.VMEM((tokens, slots), BF16),
        pltpu.VMEM((tokens, half + EXTRA), BF16),
        pltpu.VMEM((slots, half + EXTRA), BF16),
        pltpu.VMEM((2, slots, half + EXTRA), BF16),
        pltpu.VMEM((slots, 2 * ff), F32),
        pltpu.VMEM((slots, 2 * ff), BF16),
        pltpu.VMEM((slots, half), BF16),
        pltpu.VMEM((slots, half), BF16),
        pltpu.VMEM((tokens, half), BF16),
        pltpu.VMEM((tokens, half), BF16),
        dma((5,)), dma((CHUNKS,)), dma((5,)),
        dma((CHUNKS,)), dma((CHUNKS,)), dma((2,)), dma((2,)),
        dma((CHUNKS,)), dma((CHUNKS,)), dma((CHUNKS,)), dma((CHUNKS,)),
        dma((CHUNKS,)), dma((CHUNKS,)),
        dma((2,)), dma((CHUNKS,)), dma((CHUNKS,)), dma((CHUNKS,)), dma((CHUNKS,)), dma((CHUNKS,)),
        pltpu.VMEM((rows, half), BF16),
    ]
    return pl.pallas_call(
        kernel,
        out_shape=jax.ShapeDtypeStruct((rows, half), BF16),
        in_specs=[pl.BlockSpec(memory_space=pltpu.HBM)] * 9,
        out_specs=pl.BlockSpec(memory_space=pltpu.HBM),
        scratch_shapes=scratch,
        compiler_params=pltpu.CompilerParams(
            collective_id=0, has_side_effects=True, vmem_limit_bytes=60 * 1024 * 1024
        ),
        name="block",
    )(
        context, out_weight, residual, norm_gain, expert_ids.T, route_prob.T,
        w_gate, w_up, w_down,
    )


def solution(mesh):
    placed = (
        P("expert", "tensor"),
        P("tensor", "pair"),
        P(("expert", "tensor"), "pair"),
        P(),
        P(("expert", "tensor"), None),
        P(("expert", "tensor"), None),
        P(("expert", "tensor"), None, "pair"),
        P(("expert", "tensor"), None, "pair"),
        P(("expert", "tensor"), "pair", None),
    )
    return jax.shard_map(
        body, mesh=mesh, in_specs=placed, out_specs=P(("expert", "tensor"), "pair"), check_vma=False
    )
```

```python
import functools

import jax
import jax.numpy as jnp
from jax import lax
from jax.experimental import pallas as pl
from jax.experimental.pallas import tpu as pltpu
from jax.sharding import PartitionSpec as P

EPS = 1e-06
MESH = pl.DeviceIdType.MESH
BF16 = jnp.bfloat16
F32 = jnp.float32
ROWS = 16
NZ = 8
NT = 8
NQ = 16
WIDTHS = (512, 512, 512, 512)
CHUNKS = len(WIDTHS)
STARTS = tuple(sum(WIDTHS[:c]) for c in range(CHUNKS))
AHEAD = 2
WAY_OUT = ("T0", "G0", "S2", "G1", "S3", "D0", "G2", "D1", "G3", "F0", "D2", "U0", "F1", "D3", "M0", "F2", "M1", "F3", "M2", "M3")
WAY_BACK = ("P0", "P1", "P2", "X0", "P3", "Q0", "X1", "X2", "E0", "X3", "E1", "E2", "E3")
EXTRA = 128


def dot(a, b):
    return jnp.dot(a, b, preferred_element_type=F32)


def dot_nt(a, b):
    return lax.dot_general(a, b, (((1,), (1,)), ((), ())), preferred_element_type=F32)


def rows16(index):
    return pl.ds(pl.multiple_of(index * ROWS, ROWS), ROWS)


def kernel(
    ctx_hbm, ow_hbm, res_hbm, gain_hbm, ids_hbm, prob_hbm, wg_hbm, wu_hbm, wd_hbm, out_ref,
    ctx, ow, res, gain, ids, prob, wgu, wd,
    attb, ars, stream, meta, metal, table, chi, clo,
    line, disp, xs, acc, hid, outb, ret, mixb, zr,
    ld, ow_sem, w_sem,
    a_send, a_recv, m_sem, wd_sem, g_send, g_recv, d_send, d_recv, f_send, f_recv,
    h_sem, r_send, r_recv, z_send, z_recv, o_sem, result,
):
    e, t, p = lax.axis_index("expert"), lax.axis_index("tensor"), lax.axis_index("pair")
    z, x_lo = lax.rem(e, NZ), lax.div(e, NZ)
    y, x_hi = lax.div(t, 2), lax.rem(t, 2)
    x = x_hi * 2 + x_lo
    q = x_lo * NT + t
    half = ow.shape[1]
    ff = wg_hbm.shape[2]
    slots = NQ * ROWS
    tokens = NZ * ROWS
    partner = (e, t, 1 - p)

    def along(j):
        return lax.rem(z + j, NZ)

    def z_peer(j):
        return (x_lo * NZ + along(j), t, p)

    def plane_peer(j):
        px, py = lax.rem(x + lax.rem(j, 4), 4), lax.rem(y + lax.div(j, 4), 4)
        plo, pt = lax.rem(px, 2), py * 2 + lax.div(px, 2)
        return plo * NT + pt, (plo * NZ + z, pt, p)

    def each(count, fn):
        def step(j, carry):
            fn(j)
            return carry
        lax.fori_loop(1, count, step, 0)

    def remote(src, dst, send, recv, device):
        return pltpu.make_async_remote_copy(
            src_ref=src, dst_ref=dst, send_sem=send, recv_sem=recv,
            device_id=device, device_id_type=MESH,
        )

    def wait_bytes(ref, sem):
        pltpu.make_async_copy(ref, ref, sem).wait()

    def cols(c):
        return pl.ds(STARTS[c], WIDTHS[c])

    def more(c):
        return pl.ds(STARTS[c], WIDTHS[c] + (EXTRA if c == CHUNKS - 1 else 0))

    def mine(index):
        return pl.ds(pl.multiple_of(index * half, half), half)

    pending = []

    def drain(count):
        for _ in range(count):
            pending.pop(0)()

    loads = [
        pltpu.make_async_copy(ctx_hbm, ctx, ld.at[0]),
        pltpu.make_async_copy(res_hbm, res, ld.at[1]),
        pltpu.make_async_copy(gain_hbm.at[mine(p)], gain, ld.at[2]),
        pltpu.make_async_copy(ids_hbm, ids, ld.at[3]),
        pltpu.make_async_copy(prob_hbm, prob, ld.at[4]),
    ]
    ow_loads = [
        pltpu.make_async_copy(ow_hbm.at[:, cols(c)], ow.at[:, cols(c)], ow_sem.at[c])
        for c in range(CHUNKS)
    ]
    w_loads = []
    for k, side in enumerate((p, 1 - p)):
        w_loads.append(pltpu.make_async_copy(
            wg_hbm.at[0, mine(side), :], wgu.at[k, :, pl.ds(0, ff)], w_sem.at[2 * k]))
        w_loads.append(pltpu.make_async_copy(
            wu_hbm.at[0, mine(side), :], wgu.at[k, :, pl.ds(ff, ff)], w_sem.at[2 * k + 1]))
    wd_load = pltpu.make_async_copy(wd_hbm.at[0, :, mine(p)], wd.at[pl.ds(0, ff), :], w_sem.at[4])
    for copy in loads[:1] + ow_loads + loads[1:]:
        copy.start()

    barrier = pltpu.get_barrier_semaphore()
    each(NQ, lambda j: pl.semaphore_signal(barrier, inc=1, device_id=plane_peer(j)[1], device_id_type=MESH))
    each(NZ, lambda j: pl.semaphore_signal(barrier, inc=1, device_id=z_peer(j), device_id_type=MESH))
    pl.semaphore_signal(barrier, inc=1, device_id=partner, device_id_type=MESH)

    def project(c):
        ow_loads[c].wait()
        attb[:, cols(c)] = dot(ctx[...], ow[:, cols(c)]).astype(BF16)

    def scatter_heads(c):
        def send(j):
            pt = lax.rem(t + j, NT)
            remote(attb.at[rows16(pt), cols(c)], ars.at[rows16(t), cols(c)],
                   a_send.at[c], a_recv.at[c], (e, pt, p)).start()
        each(NT, send)
        pending.append(lambda: wait_bytes(ars.at[pl.ds(0, (NT - 1) * ROWS), cols(c)], a_send.at[c]))

    loads[0].wait()
    project(0)
    pl.semaphore_wait(barrier, NZ - 1 + NQ - 1 + 1)
    scatter_heads(0)
    for c in range(1, AHEAD):
        project(c)
        scatter_heads(c)
    for copy in w_loads + [wd_load]:
        copy.start()

    for copy in loads[1:]:
        copy.wait()
    weights = prob[...] / jnp.sum(prob[...], axis=0, keepdims=True)
    named = ids[...]
    experts = lax.broadcasted_iota(jnp.int32, (128, ROWS), 0)
    mark = jnp.zeros((128, ROWS), F32)
    spread = jnp.zeros((128, ROWS), F32)
    for k in range(named.shape[0]):
        same = experts == named[k:k + 1, :]
        mark = jnp.where(same, 1.0, mark)
        spread = jnp.where(same, weights[k:k + 1, :], spread)
    before = lax.broadcasted_iota(jnp.int32, (ROWS, ROWS), 1)
    after = lax.broadcasted_iota(jnp.int32, (ROWS, ROWS), 0)
    earlier = (before < after).astype(F32).astype(BF16)
    same_row = (before == after).astype(F32).astype(BF16)
    mark = mark.astype(BF16)
    high = spread.astype(BF16)
    low = (spread - high.astype(F32)).astype(BF16)
    meta[0] = (dot_nt(same_row, mark) * (1.0 + dot_nt(earlier, mark))).astype(BF16)
    meta[1] = dot_nt(same_row, high).astype(BF16)
    meta[2] = dot_nt(same_row, low).astype(BF16)
    metal[:, rows16(z), :] = meta[...]
    each(NZ, lambda j: remote(meta, metal.at[:, rows16(z), :], m_sem.at[0], m_sem.at[1], z_peer(j)).start())
    pending.append(lambda: wait_bytes(metal.at[:, pl.ds(0, (NZ - 1) * ROWS), :], m_sem.at[0]))
    wd_swap = remote(wd_hbm.at[0, :, mine(1 - p)], wd.at[pl.ds(ff, ff), :], wd_sem.at[0], wd_sem.at[1], partner)
    wd_swap.start()
    pending.append(wd_swap.wait_send)

    def expert_of(row):
        place = lax.shift_right_logical(row, 4)
        return (lax.shift_right_logical(place, 3) * (NZ * NT) + z * NT + (place & (NT - 1)))

    def fits(row, token, codes):
        wanted = ((row & 1) + 1).astype(F32)
        same = (lax.shift_right_logical(row, 1) & (NZ - 1)) == lax.shift_right_logical(token, 4)
        return same & (codes == wanted)

    def iota(rows, columns, axis):
        return lax.broadcasted_iota(jnp.int32, (rows, columns), axis)

    def picker():
        return (iota(slots, 128, 1) == expert_of(iota(slots, 128, 0))).astype(F32).astype(BF16)

    def down_table():
        wait_bytes(metal.at[:, pl.ds(0, (NZ - 1) * ROWS), :], m_sem.at[1])
        codes = dot_nt(picker(), metal[0])
        chosen = fits(iota(slots, tokens, 0), iota(slots, tokens, 1), codes)
        table[...] = jnp.where(chosen, 1.0, 0.0).astype(BF16)

    def up_tables():
        pick = picker()
        chosen = fits(iota(tokens, slots, 1), iota(tokens, slots, 0), dot_nt(metal[0], pick))
        chi[...] = jnp.where(chosen, dot_nt(metal[1], pick), 0.0).astype(BF16)
        clo[...] = jnp.where(chosen, dot_nt(metal[2], pick), 0.0).astype(BF16)

    squares = [jnp.zeros((ROWS, 1), F32)]

    def gather_heads(c):
        ars[rows16(t), cols(c)] = attb[rows16(t), cols(c)]
        wait_bytes(ars.at[pl.ds(0, (NT - 1) * ROWS), cols(c)], a_recv.at[c])
        total = res[:, cols(c)].astype(F32)
        heads = ars[0:ROWS, cols(c)].astype(F32)
        for k in range(1, NT):
            heads += ars[k * ROWS:(k + 1) * ROWS, cols(c)].astype(F32)
        part = (total + heads).astype(BF16)
        stream[:, cols(c)] = part
        wide = part.astype(F32)
        squares[0] = squares[0] + jnp.sum(wide * wide, axis=1, keepdims=True)
        line[rows16(z), cols(c)] = (wide * gain[cols(c)].astype(F32)[None, :]).astype(BF16)
        if c == CHUNKS - 1:
            top = squares[0].astype(BF16).astype(F32)
            middle = (squares[0] - top).astype(BF16).astype(F32)
            lane = iota(ROWS, EXTRA, 1)
            parts = jnp.where(lane == 0, top, jnp.where(lane == 1, middle, squares[0] - top - middle))
            line[rows16(z), pl.ds(half, EXTRA)] = jnp.where(lane < 3, parts, 0.0).astype(BF16)
        each(NZ, lambda j: remote(line.at[rows16(z), more(c)], line.at[rows16(z), more(c)],
                                  g_send.at[c], g_recv.at[c], z_peer(lax.rem(j * 3, NZ))).start())
        pending.append(lambda: wait_bytes(line.at[pl.ds(0, tokens - ROWS), more(c)], g_send.at[c]))

    def dispatch(c):
        wait_bytes(line.at[pl.ds(0, tokens - ROWS), more(c)], g_recv.at[c])
        disp[:, more(c)] = dot(table[...], line[:, more(c)]).astype(BF16)

        def send(j):
            pq, device = plane_peer(j)
            remote(disp.at[rows16(pq), more(c)], xs.at[0, rows16(q), more(c)],
                   d_send.at[c], d_recv.at[c], device).start()
        each(NQ, send)
        pending.append(lambda: wait_bytes(xs.at[0, pl.ds(0, slots - ROWS), more(c)], d_send.at[c]))
        xs[0, rows16(q), more(c)] = disp[rows16(q), more(c)]

    forwards = [
        remote(xs.at[0, :, more(c)], xs.at[1, :, more(c)], f_send.at[c], f_recv.at[c], partner)
        for c in range(CHUNKS)
    ]

    def forward(c):
        wait_bytes(xs.at[0, pl.ds(0, slots - ROWS), more(c)], d_recv.at[c])
        forwards[c].start()
        pending.append(forwards[c].wait_send)

    def multiply(c):
        own = dot(xs[0, :, cols(c)], wgu[0, cols(c), :])
        forwards[c].wait_recv()
        both = own + dot(xs[1, :, cols(c)], wgu[1, cols(c), :])
        if c == 0:
            acc[...] = both
        else:
            acc[...] += both

    def head_start(c):
        project(c)
        scatter_heads(c)

    def tables():
        up_tables()
        for copy in w_loads:
            copy.wait()

    steps = {
        "S": head_start, "G": gather_heads, "D": dispatch, "F": forward, "M": multiply,
        "T": lambda c: down_table(), "U": lambda c: tables(),
    }
    for name in WAY_OUT:
        steps[name[0]](int(name[1]))

    sums = jnp.sum(xs[0, :, pl.ds(half, EXTRA)].astype(F32) + xs[1, :, pl.ds(half, EXTRA)].astype(F32),
                   axis=1, keepdims=True)
    scale = lax.rsqrt(sums * (1.0 / (2 * half)) + EPS)
    gate, up = acc[:, 0:ff] * scale, acc[:, ff:2 * ff] * scale
    hid[:, 0:ff] = (gate / (1.0 + jnp.exp(-gate)) * up).astype(BF16)
    hid_swap = remote(hid.at[:, pl.ds(0, ff)], hid.at[:, pl.ds(ff, ff)], h_sem.at[0], h_sem.at[1], partner)
    hid_swap.start()
    pending.append(hid_swap.wait_send)
    wd_load.wait()
    wd_swap.wait_recv()
    hid_swap.wait_recv()
    early = len(pending)

    def produce(c):
        outb[:, cols(c)] = dot(hid[...], wd[:, cols(c)]).astype(BF16)

        def send(j):
            pq, device = plane_peer(j)
            remote(outb.at[rows16(pq), cols(c)], ret.at[rows16(q), cols(c)],
                   r_send.at[c], r_recv.at[c], device).start()
        each(NQ, send)
        pending.append(lambda: wait_bytes(ret.at[pl.ds(0, slots - ROWS), cols(c)], r_send.at[c]))
        ret[rows16(q), cols(c)] = outb[rows16(q), cols(c)]

    def mix(c):
        wait_bytes(ret.at[pl.ds(0, slots - ROWS), cols(c)], r_recv.at[c])
        mixb[:, cols(c)] = (dot(chi[...], ret[:, cols(c)]) + dot(clo[...], ret[:, cols(c)])).astype(BF16)

        def send(j):
            j = lax.rem(j * 3, NZ)
            remote(mixb.at[rows16(along(j)), cols(c)], zr.at[rows16(z), cols(c)],
                   z_send.at[c], z_recv.at[c], z_peer(j)).start()
        each(NZ, send)
        pending.append(lambda: wait_bytes(zr.at[pl.ds(0, tokens - ROWS), cols(c)], z_send.at[c]))
        zr[rows16(z), cols(c)] = mixb[rows16(z), cols(c)]

    def finish(c):
        wait_bytes(zr.at[pl.ds(0, tokens - ROWS), cols(c)], z_recv.at[c])
        total = stream[:, cols(c)].astype(F32)
        for k in range(NZ):
            total += zr[k * ROWS:(k + 1) * ROWS, cols(c)].astype(F32)
        result[:, cols(c)] = total.astype(BF16)
        leave = pltpu.make_async_copy(result.at[:, cols(c)], out_ref.at[:, cols(c)], o_sem.at[c])
        leave.start()
        pending.append(leave.wait)

    steps = {"P": produce, "X": mix, "E": finish, "Q": lambda c: drain(early if c == 0 else CHUNKS)}
    for name in WAY_BACK:
        steps[name[0]](int(name[1]))

    drain(len(pending))


def body(context, out_weight, residual, norm_gain, expert_ids, route_prob, w_gate, w_up, w_down):
    rows, half = residual.shape
    group, depth = context.shape
    ff = w_gate.shape[2]
    slots, tokens = NQ * ROWS, NZ * ROWS
    dma = pltpu.SemaphoreType.DMA
    scratch = [
        pltpu.VMEM((group, depth), BF16),
        pltpu.VMEM((depth, half), BF16),
        pltpu.VMEM((rows, half), BF16),
        pltpu.VMEM((half,), BF16),
        pltpu.VMEM(expert_ids.shape[::-1], jnp.int32),
        pltpu.VMEM(route_prob.shape[::-1], F32),
        pltpu.VMEM((2, half, 2 * ff), BF16),
        pltpu.VMEM((2 * ff, half), BF16),
        pltpu.VMEM((group, half), BF16),
        pltpu.VMEM((group, half), BF16),
        pltpu.VMEM((rows, half), BF16),
        pltpu.VMEM((3, rows, 128), BF16),
        pltpu.VMEM((3, tokens, 128), BF16),
        pltpu.VMEM((slots, tokens), BF16),
        pltpu.VMEM((tokens, slots), BF16),
        pltpu.VMEM((tokens, slots), BF16),
        pltpu.VMEM((tokens, half + EXTRA), BF16),
        pltpu.VMEM((slots, half + EXTRA), BF16),
        pltpu.VMEM((2, slots, half + EXTRA), BF16),
        pltpu.VMEM((slots, 2 * ff), F32),
        pltpu.VMEM((slots, 2 * ff), BF16),
        pltpu.VMEM((slots, half), BF16),
        pltpu.VMEM((slots, half), BF16),
        pltpu.VMEM((tokens, half), BF16),
        pltpu.VMEM((tokens, half), BF16),
        dma((5,)), dma((CHUNKS,)), dma((5,)),
        dma((CHUNKS,)), dma((CHUNKS,)), dma((2,)), dma((2,)),
        dma((CHUNKS,)), dma((CHUNKS,)), dma((CHUNKS,)), dma((CHUNKS,)),
        dma((CHUNKS,)), dma((CHUNKS,)),
        dma((2,)), dma((CHUNKS,)), dma((CHUNKS,)), dma((CHUNKS,)), dma((CHUNKS,)), dma((CHUNKS,)),
        pltpu.VMEM((rows, half), BF16),
    ]
    return pl.pallas_call(
        kernel,
        out_shape=jax.ShapeDtypeStruct((rows, half), BF16),
        in_specs=[pl.BlockSpec(memory_space=pltpu.HBM)] * 9,
        out_specs=pl.BlockSpec(memory_space=pltpu.HBM),
        scratch_shapes=scratch,
        compiler_params=pltpu.CompilerParams(
            collective_id=0, has_side_effects=True, vmem_limit_bytes=60 * 1024 * 1024
        ),
        name="block",
    )(
        context, out_weight, residual, norm_gain, expert_ids.T, route_prob.T,
        w_gate, w_up, w_down,
    )


def solution(mesh):
    placed = (
        P("expert", "tensor"),
        P("tensor", "pair"),
        P(("expert", "tensor"), "pair"),
        P(),
        P(("expert", "tensor"), None),
        P(("expert", "tensor"), None),
        P(("expert", "tensor"), None, "pair"),
        P(("expert", "tensor"), None, "pair"),
        P(("expert", "tensor"), "pair", None),
    )
    return jax.shard_map(
        body, mesh=mesh, in_specs=placed, out_specs=P(("expert", "tensor"), "pair"), check_vma=False
    )
```
